32 devices in a mesh: gx: 8 (over z, y), gy: 4 (over x, core).
Axes of the slice: x: 2, y: 2, z: 4, core: 2. Of those that a mesh axis runs over, the one named last changes fastest.
Arguments:
- force: float32 [32, 1024, 1024], P(None, 'gx', 'gy'), may hold values from -6 to 6
- drag: float32 [32], replicated, may hold values from 0.5 to 2
Outputs:
- velocity: float32 [32, 1024, 1024], P(None, 'gx', 'gy')
The draws below stay inside these ranges and needn't reach their ends.
All inputs are finite; a program needn't handle non-finite values.
Results may differ from the reference program's by a relative error of at most 0.0003.
Values sent between devices are 32-bit elements; how exact they have to be, the bound alone decides.
A program may use at most 192 MiB of HBM per device.

```python
import math
import jax
import jax.numpy as jnp

NX = 1024
NY = 1024
NZ = 32


def draw_force(key, part):
    key = jax.random.fold_in(key, 7)
    streams = jax.random.split(key, 5)
    x_cells = jnp.arange(NX, dtype=jnp.int32)
    y_cells = jnp.arange(NY, dtype=jnp.int32)
    alternate = (1 - 2 * (x_cells % 2)).astype(jnp.float32)
    x_phase = jax.random.uniform(streams[2], (NZ, 1, 1), jnp.float32, 0.0, 2.0 * math.pi)
    strength = jax.random.uniform(streams[3], (NZ, 1, 1), jnp.float32, 0.5, 1.0)
    x_angle = x_cells.astype(jnp.float32)[None, :, None] * (2.0 * math.pi / NX)
    envelope = strength * (0.6 + 0.4 * jnp.cos(x_angle + x_phase))
    y_phase = jax.random.uniform(streams[4], (NZ, 1, 1), jnp.float32, 0.0, 2.0 * math.pi)
    y_steps = (y_cells * (NY // 16) % NY).astype(jnp.float32)
    y_wave = jnp.cos(y_steps[None, None, :] * (2.0 * math.pi / NY) + y_phase)
    nyquist = alternate[None, :, None] * envelope * y_wave
    jitter = 0.5 * jax.random.normal(streams[0], (NZ, NX, NY), jnp.float32)
    profile = 3.5 * jax.random.normal(streams[1], (NZ, NX, 1), jnp.float32)
    combined = jitter + profile + 1.5 * nyquist
    return jnp.clip(combined, -6.0, 6.0)


def setup_inputs(seed: int = 0) -> dict:
    arg_keys = jax.random.split(jax.random.key(seed), 3)
    force = draw_force(jax.random.fold_in(arg_keys[2], 71), 0)
    drag = jnp.clip(jnp.exp(jax.random.uniform(arg_keys[1], (NZ,), jnp.float32, math.log(0.5), math.log(2.0))), 0.5, 2.0)
    return {"force": force, "drag": drag}


def green_table(drag):
    pos_x = jnp.arange(NX, dtype=jnp.int32)
    pos_y = jnp.arange(NY, dtype=jnp.int32)
    mode_x = jnp.where(pos_x < NX // 2, pos_x, pos_x - NX).astype(jnp.float32)
    mode_y = jnp.where(pos_y < NY // 2, pos_y, pos_y - NY).astype(jnp.float32)
    square = mode_x[:, None] ** 2 + mode_y[None, :] ** 2
    project = 1.0 - mode_x[:, None] ** 2 / jnp.maximum(square, 1.0)
    denom = drag[:, None, None] + (16.0 / (NX * NY)) * square[None, :, :]
    return project[None, :, :] / denom


def reference(force, drag):
    spectrum = jnp.fft.fft2(force, axes=(1, 2))
    scaled = spectrum * green_table(drag)
    result = jnp.real(jnp.fft.ifft2(scaled, axes=(1, 2)))
    return result.astype(force.dtype)
```

```python
import functools
import math

import jax
import jax.numpy as jnp
import numpy as np
from jax import lax
from jax.experimental import pallas as pl
from jax.experimental.pallas import tpu as pltpu
from jax.sharding import PartitionSpec as P

HIGH = lax.Precision.HIGHEST
MESH = pl.DeviceIdType.MESH
CHUNKS = 4
TILE = 256


def real_modes(length):
    half = length // 2
    row = np.arange(length)
    mode = np.where(row <= half, row, row - half)
    phase = np.outer(mode, np.arange(length)) % length
    angle = phase * (2.0 * np.pi / length)
    table = np.where((row <= half)[:, None], np.cos(angle), np.sin(angle))
    weight = np.where((row == 0) | (row == half), 1.0, 2.0) / length
    return table * np.sqrt(weight)[:, None]


def two_parts(table):
    high = table.astype(jnp.bfloat16)
    low = (table - high.astype(np.float64)).astype(jnp.bfloat16)
    return high, low


def split(value):
    high = value.astype(jnp.bfloat16)
    return high, (value - high.astype(jnp.float32)).astype(jnp.bfloat16)


def product(a_high, a_low, b_high, b_low):
    dot = functools.partial(jnp.dot, preferred_element_type=jnp.float32)
    return dot(a_high, b_high) + (dot(a_high, b_low) + dot(a_low, b_high))


def plane_kernel(
    nx, ny, force, drag, tables_in, turned_in, out, plane, green, table, turned, part, lines, modes,
    table_sem, send, recv, back_send, back_recv,
):
    gx, gy = lax.axis_index("gx"), lax.axis_index("gy")
    me = gx * ny + gy
    devices = nx * ny
    chunks, rows = plane.shape[1], plane.shape[2]
    width = force.shape[2]
    length = plane.shape[3]
    len_x = nx * chunks * rows
    count = nx * rows

    def peer(i):
        px = lax.rem(gx + (nx - 1 - lax.rem(i, nx)), nx)
        py = lax.rem(gy + (ny - 1 - i // nx), ny)
        return px, py

    def columns(j, size):
        return pl.ds(pl.multiple_of(j * size, size), size)

    def band(c):
        return pl.ds(pl.multiple_of(c * rows, rows), rows)

    loads = [
        pltpu.make_async_copy(tables_in, table, table_sem.at[0]),
        pltpu.make_async_copy(turned_in, turned, table_sem.at[1]),
    ]
    for load in loads:
        load.start()

    barrier = pltpu.get_barrier_semaphore()

    @pl.loop(0, devices - 1)
    def _(i):
        pl.semaphore_signal(barrier, inc=1, device_id=peer(i), device_id_type=MESH)

    pl.semaphore_wait(barrier, devices - 1)

    @pl.loop(0, chunks)
    def _(c):
        @pl.loop(0, devices - 1)
        def _(i):
            px, py = peer(i)
            pltpu.make_async_remote_copy(
                src_ref=force.at[px * ny + py, band(c)],
                dst_ref=plane.at[gx, c, :, columns(gy, width)],
                send_sem=send.at[c],
                recv_sem=recv.at[c],
                device_id=(px, py),
                device_id_type=MESH,
            ).start()

        pltpu.make_async_copy(
            force.at[me, band(c)], plane.at[gx, c, :, columns(gy, width)], recv.at[c]
        ).start()

    friction = drag[me]

    @pl.loop(0, len_x // TILE)
    def _(i):
        first = lax.broadcasted_iota(jnp.int32, (TILE, length), 0) + i * TILE
        second = lax.broadcasted_iota(jnp.int32, (TILE, length), 1)
        mode_x = jnp.where(first <= len_x // 2, first, first - len_x // 2).astype(jnp.float32)
        mode_y = jnp.where(second <= length // 2, second, second - length // 2).astype(jnp.float32)
        square_x = mode_x * mode_x
        square = square_x + mode_y * mode_y
        floor = jnp.maximum(square, 1.0)
        denom = friction + 16.0 / (len_x * length) * square
        green[columns(i, TILE), :] = (floor - square_x) / (floor * denom)

    for load in loads:
        load.wait()

    @pl.loop(0, chunks)
    def _(c):
        pltpu.make_async_copy(plane.at[:, c], plane.at[:, c], recv.at[c]).wait()
        high, low = split(plane[:, c].reshape(count, length))
        part[0] = high
        part[1] = low

        @pl.loop(0, length // TILE)
        def _(j):
            cols = columns(j, TILE)
            result = product(
                part[0],
                part[1],
                turned[0, :, :, :, cols].reshape(length, TILE),
                turned[1, :, :, :, cols].reshape(length, TILE),
            )
            high, low = split(result)
            lines[0, :, c, :, cols] = high.reshape(nx, rows, TILE)
            lines[1, :, c, :, cols] = low.reshape(nx, rows, TILE)

    @pl.loop(0, length // TILE)
    def _(j):
        cols = columns(j, TILE)

        @pl.loop(0, len_x // (2 * TILE))
        def _(i):
            band_i = columns(i, 2 * TILE)
            result = product(
                table[0, band_i, :],
                table[1, band_i, :],
                lines[0, :, :, :, cols].reshape(len_x, TILE),
                lines[1, :, :, :, cols].reshape(len_x, TILE),
            )
            high, low = split(result * green[band_i, cols])
            modes[0, band_i, cols] = high
            modes[1, band_i, cols] = low

    @pl.loop(0, chunks)
    def _(c):
        @pl.loop(0, length // TILE)
        def _(j):
            cols = columns(j, TILE)
            result = product(
                turned[0, :, c].reshape(count, len_x),
                turned[1, :, c].reshape(count, len_x),
                modes[0, :, cols],
                modes[1, :, cols],
            )
            high, low = split(result)
            part[0, :, cols] = high
            part[1, :, cols] = low

        @pl.loop(0, length // TILE)
        def _(j):
            cols = columns(j, TILE)
            result = product(part[0], part[1], table[0, :, cols], table[1, :, cols])
            plane[:, c, :, cols] = result.reshape(nx, rows, TILE)

        @pl.loop(0, devices - 1)
        def _(i):
            px, py = peer(i)
            pltpu.make_async_remote_copy(
                src_ref=plane.at[px, c, :, columns(py, width)],
                dst_ref=out.at[me, band(c)],
                send_sem=back_send.at[c],
                recv_sem=back_recv.at[c],
                device_id=(px, py),
                device_id_type=MESH,
            ).start()

        pltpu.make_async_copy(
            plane.at[gx, c, :, columns(gy, width)], out.at[me, band(c)], back_recv.at[c]
        ).start()

    @pl.loop(0, chunks)
    def _(c):
        sent = force.at[pl.ds(0, devices - 1), band(c)]
        pltpu.make_async_copy(sent, sent, send.at[c]).wait()
        pltpu.make_async_copy(sent, sent, back_send.at[c]).wait()
        landed = out.at[:, band(c)]
        pltpu.make_async_copy(landed, landed, back_recv.at[c]).wait()


def by_planes(force, drag):
    nx, ny = lax.axis_size("gx"), lax.axis_size("gy")
    planes, width_x, width_y = force.shape
    length = width_x * nx
    rows = width_x // CHUNKS
    modes = real_modes(length)
    table = np.stack(two_parts(modes))
    turned = np.stack(two_parts(modes.T)).reshape(2, nx, CHUNKS, rows, length)
    anywhere = pl.BlockSpec(memory_space=pl.ANY)
    bf16, f32 = jnp.bfloat16, jnp.float32
    return pl.pallas_call(
        functools.partial(plane_kernel, nx, ny),
        out_shape=jax.ShapeDtypeStruct(force.shape, force.dtype),
        in_specs=[anywhere, pl.BlockSpec(memory_space=pltpu.SMEM), anywhere, anywhere],
        out_specs=anywhere,
        scratch_shapes=[
            pltpu.VMEM((nx, CHUNKS, rows, length), f32),
            pltpu.VMEM((length, length), f32),
            pltpu.VMEM((2, length, length), bf16),
            pltpu.VMEM((2, nx, CHUNKS, rows, length), bf16),
            pltpu.VMEM((2, nx * rows, length), bf16),
            pltpu.VMEM((2, nx, CHUNKS, rows, length), bf16),
            pltpu.VMEM((2, length, length), bf16),
            pltpu.SemaphoreType.DMA((2,)),
            pltpu.SemaphoreType.DMA((CHUNKS,)),
            pltpu.SemaphoreType.DMA((CHUNKS,)),
            pltpu.SemaphoreType.DMA((CHUNKS,)),
            pltpu.SemaphoreType.DMA((CHUNKS,)),
        ],
        compiler_params=pltpu.CompilerParams(
            collective_id=0, has_side_effects=True, vmem_limit_bytes=48 * 1024 * 1024
        ),
        cost_estimate=pl.CostEstimate(
            flops=24 * length**3, bytes_accessed=8 * force.size, transcendentals=0
        ),
    )(force, drag, jnp.asarray(table), jnp.asarray(turned))


def tables(row_pos, col_pos, length):
    phase = row_pos[:, None] * col_pos[None, :] % length
    angle = phase.astype(jnp.float32) * (2.0 * math.pi / length)
    return (jnp.cos(angle), jnp.sin(angle))


def green_block(drag, x_pos, y_pos, len_x, len_y):
    mode_x = jnp.where(x_pos < len_x // 2, x_pos, x_pos - len_x).astype(jnp.float32)
    mode_y = jnp.where(y_pos < len_y // 2, y_pos, y_pos - len_y).astype(jnp.float32)
    square = mode_x[:, None] ** 2 + mode_y[None, :] ** 2
    project = 1.0 - mode_x[:, None] ** 2 / jnp.maximum(square, 1.0)
    denom = drag[:, None, None] + 16.0 / (len_x * len_y) * square[None, :, :]
    return project[None, :, :] / denom


def swap_x(stacked, sign):

    def work(piece):
        length = piece.shape[2]
        index = lax.iota(jnp.int32, length)
        cosine, sine_tab = tables(index, index, length)
        first = piece[0]
        if piece.shape[0] == 2:
            second = piece[1]
            real_part = jnp.einsum(
                "kx,zxq->zkq", cosine, first, precision=HIGH
            ) - sign * jnp.einsum("kx,zxq->zkq", sine_tab, second, precision=HIGH)
            imag_part = sign * jnp.einsum(
                "kx,zxq->zkq", sine_tab, first, precision=HIGH
            ) + jnp.einsum("kx,zxq->zkq", cosine, second, precision=HIGH)
        else:
            real_part = jnp.einsum("kx,zxq->zkq", cosine, first, precision=HIGH)
            imag_part = sign * jnp.einsum("kx,zxq->zkq", sine_tab, first, precision=HIGH)
        outgoing = jnp.stack([real_part, imag_part], 0)
        return lax.all_to_all(outgoing, "gx", split_axis=2, concat_axis=3, tiled=True)

    return work(lax.all_to_all(stacked, "gx", split_axis=3, concat_axis=2, tiled=True))


def swap_y(stacked, sign, keep_imag):

    def work(piece):
        length = piece.shape[3]
        index = lax.iota(jnp.int32, length)
        cosine, sine_tab = tables(index, index, length)
        first = piece[0]
        second = piece[1]
        real_part = jnp.einsum("ky,zpy->zpk", cosine, first, precision=HIGH) - sign * jnp.einsum(
            "ky,zpy->zpk", sine_tab, second, precision=HIGH
        )
        if keep_imag:
            imag_part = sign * jnp.einsum(
                "ky,zpy->zpk", sine_tab, first, precision=HIGH
            ) + jnp.einsum("ky,zpy->zpk", cosine, second, precision=HIGH)
            outgoing = jnp.stack([real_part, imag_part], 0)
        else:
            outgoing = real_part[None]
        return lax.all_to_all(outgoing, "gy", split_axis=3, concat_axis=2, tiled=True)

    return work(lax.all_to_all(stacked, "gy", split_axis=2, concat_axis=3, tiled=True))


def on_device(force, drag):
    planes, width_x, width_y = force.shape
    len_x = width_x * lax.axis_size("gx")
    len_y = width_y * lax.axis_size("gy")
    whole_planes = planes == lax.axis_size("gx") * lax.axis_size("gy") and len_x == len_y
    if whole_planes and width_x % (16 * CHUNKS) == 0 and width_y % TILE == 0:
        return by_planes(force, drag)
    x_pos = lax.axis_index("gx") * width_x + lax.iota(jnp.int32, width_x)
    y_pos = lax.axis_index("gy") * width_y + lax.iota(jnp.int32, width_y)
    spectrum = swap_x(force[None], -1.0)
    green = green_block(drag, x_pos, y_pos, len_x, len_y)
    spectrum = swap_y(spectrum, -1.0, True)
    scaled = spectrum * green[None]
    inverse = swap_x(scaled, 1.0)
    inverse = swap_y(inverse, 1.0, False)
    result = inverse[0] * (1.0 / (len_x * len_y))
    return result


def solution(mesh):
    placed = (P(None, "gx", "gy"), P())
    return jax.shard_map(
        on_device, mesh=mesh, in_specs=placed, out_specs=P(None, "gx", "gy"), check_vma=False
    )
```

```python
import functools
import math

import jax
import jax.numpy as jnp
import numpy as np
from jax import lax
from jax.experimental import pallas as pl
from jax.experimental.pallas import tpu as pltpu
from jax.sharding import PartitionSpec as P

HIGH = lax.Precision.HIGHEST
MESH = pl.DeviceIdType.MESH
CHUNKS = 8
TILE = 256


def real_modes(length):
    half = length // 2
    row = np.arange(length)
    mode = np.where(row <= half, row, row - half)
    phase = np.outer(mode, np.arange(length)) % length
    angle = phase * (2.0 * np.pi / length)
    table = np.where((row <= half)[:, None], np.cos(angle), np.sin(angle))
    weight = np.where((row == 0) | (row == half), 1.0, 2.0) / length
    return table * np.sqrt(weight)[:, None]


def two_parts(table):
    high = table.astype(jnp.bfloat16)
    low = (table - high.astype(np.float64)).astype(jnp.bfloat16)
    return high, low


def split(value):
    high = value.astype(jnp.bfloat16)
    return high, (value - high.astype(jnp.float32)).astype(jnp.bfloat16)


def product(a_high, a_low, b_high, b_low):
    dot = functools.partial(jnp.dot, preferred_element_type=jnp.float32)
    return dot(a_high, b_high) + (dot(a_high, b_low) + dot(a_low, b_high))


def plane_kernel(
    nx, ny, force, drag, tables_in, turned_in, pieces_in, out, plane, green, table, turned, pieces, part, lines,
    total, modes,
    table_sem, send, recv, back_send, back_recv,
):
    gx, gy = lax.axis_index("gx"), lax.axis_index("gy")
    me = gx * ny + gy
    devices = nx * ny
    chunks, rows = plane.shape[1], plane.shape[2]
    width = force.shape[2]
    length = plane.shape[3]
    len_x = nx * chunks * rows
    count = nx * rows

    def peer(i):
        px = lax.rem(gx + (nx - 1 - lax.rem(i, nx)), nx)
        py = lax.rem(gy + (ny - 1 - i // nx), ny)
        return px, py

    def columns(j, size):
        return pl.ds(pl.multiple_of(j * size, size), size)

    def band(c):
        return pl.ds(pl.multiple_of(c * rows, rows), rows)

    loads = [
        pltpu.make_async_copy(tables_in, table, table_sem.at[0]),
        pltpu.make_async_copy(turned_in, turned, table_sem.at[1]),
        pltpu.make_async_copy(pieces_in, pieces, table_sem.at[2]),
    ]
    for load in loads:
        load.start()

    barrier = pltpu.get_barrier_semaphore()

    @pl.loop(0, devices - 1)
    def _(i):
        pl.semaphore_signal(barrier, inc=1, device_id=peer(i), device_id_type=MESH)

    pl.semaphore_wait(barrier, devices - 1)

    @pl.loop(0, chunks)
    def _(c):
        @pl.loop(0, devices - 1)
        def _(i):
            px, py = peer(i)
            pltpu.make_async_remote_copy(
                src_ref=force.at[px * ny + py, band(c)],
                dst_ref=plane.at[gx, c, :, columns(gy, width)],
                send_sem=send.at[c],
                recv_sem=recv.at[c],
                device_id=(px, py),
                device_id_type=MESH,
            ).start()

        pltpu.make_async_copy(
            force.at[me, band(c)], plane.at[gx, c, :, columns(gy, width)], recv.at[c]
        ).start()

    friction = drag[me]

    @pl.loop(0, len_x // TILE)
    def _(i):
        first = lax.broadcasted_iota(jnp.int32, (TILE, length), 0) + i * TILE
        second = lax.broadcasted_iota(jnp.int32, (TILE, length), 1)
        mode_x = jnp.where(first <= len_x // 2, first, first - len_x // 2).astype(jnp.float32)
        mode_y = jnp.where(second <= length // 2, second, second - length // 2).astype(jnp.float32)
        square_x = mode_x * mode_x
        square = square_x + mode_y * mode_y
        floor = jnp.maximum(square, 1.0)
        denom = friction + 16.0 / (len_x * length) * square
        total[columns(i, TILE), :] = jnp.zeros((TILE, length), jnp.float32)
        green[columns(i, TILE), :] = (floor - square_x) / (floor * denom)

    for load in loads:
        load.wait()

    def arrive(c, last):
        pltpu.make_async_copy(plane.at[:, c], plane.at[:, c], recv.at[c]).wait()
        high, low = split(plane[:, c].reshape(count, length))
        part[0] = high
        part[1] = low

        @pl.loop(0, length // TILE)
        def _(j):
            cols = columns(j, TILE)
            result = product(
                part[0],
                part[1],
                turned[0, :, :, :, cols].reshape(length, TILE),
                turned[1, :, :, :, cols].reshape(length, TILE),
            )
            high, low = split(result)
            lines[0, :, cols] = high
            lines[1, :, cols] = low

        @pl.loop(0, length // TILE)
        def _(j):
            cols = columns(j, TILE)

            @pl.loop(0, len_x // (2 * TILE))
            def _(i):
                band_i = columns(i, 2 * TILE)
                result = total[band_i, cols] + product(
                    pieces[0, c, band_i, :], pieces[1, c, band_i, :], lines[0, :, cols], lines[1, :, cols]
                )
                if last:
                    high, low = split(result * green[band_i, cols])
                    modes[0, band_i, cols] = high
                    modes[1, band_i, cols] = low
                else:
                    total[band_i, cols] = result

    @pl.loop(0, chunks - 1)
    def _(c):
        arrive(c, False)

    arrive(chunks - 1, True)

    @pl.loop(0, chunks)
    def _(c):
        @pl.loop(0, length // TILE)
        def _(j):
            cols = columns(j, TILE)
            result = product(
                turned[0, :, c].reshape(count, len_x),
                turned[1, :, c].reshape(count, len_x),
                modes[0, :, cols],
                modes[1, :, cols],
            )
            high, low = split(result)
            part[0, :, cols] = high
            part[1, :, cols] = low

        @pl.loop(0, length // TILE)
        def _(j):
            cols = columns(j, TILE)
            result = product(part[0], part[1], table[0, :, cols], table[1, :, cols])
            plane[:, c, :, cols] = result.reshape(nx, rows, TILE)

        @pl.loop(0, devices - 1)
        def _(i):
            px, py = peer(i)
            pltpu.make_async_remote_copy(
                src_ref=plane.at[px, c, :, columns(py, width)],
                dst_ref=out.at[me, band(c)],
                send_sem=back_send.at[c],
                recv_sem=back_recv.at[c],
                device_id=(px, py),
                device_id_type=MESH,
            ).start()

        pltpu.make_async_copy(
            plane.at[gx, c, :, columns(gy, width)], out.at[me, band(c)], back_recv.at[c]
        ).start()

    @pl.loop(0, chunks)
    def _(c):
        sent = force.at[pl.ds(0, devices - 1), band(c)]
        pltpu.make_async_copy(sent, sent, send.at[c]).wait()
        pltpu.make_async_copy(sent, sent, back_send.at[c]).wait()
        landed = out.at[:, band(c)]
        pltpu.make_async_copy(landed, landed, back_recv.at[c]).wait()


def by_planes(force, drag):
    nx, ny = lax.axis_size("gx"), lax.axis_size("gy")
    planes, width_x, width_y = force.shape
    length = width_x * nx
    rows = width_x // CHUNKS
    modes = real_modes(length)
    table = np.stack(two_parts(modes))
    turned = np.stack(two_parts(modes.T)).reshape(2, nx, CHUNKS, rows, length)
    pieces = table.reshape(2, length, nx, CHUNKS, rows).transpose(0, 3, 1, 2, 4).reshape(2, CHUNKS, length, nx * rows)
    anywhere = pl.BlockSpec(memory_space=pl.ANY)
    bf16, f32 = jnp.bfloat16, jnp.float32
    return pl.pallas_call(
        functools.partial(plane_kernel, nx, ny),
        out_shape=jax.ShapeDtypeStruct(force.shape, force.dtype),
        in_specs=[anywhere, pl.BlockSpec(memory_space=pltpu.SMEM), anywhere, anywhere, anywhere],
        out_specs=anywhere,
        scratch_shapes=[
            pltpu.VMEM((nx, CHUNKS, rows, length), f32),
            pltpu.VMEM((length, length), f32),
            pltpu.VMEM((2, length, length), bf16),
            pltpu.VMEM((2, nx, CHUNKS, rows, length), bf16),
            pltpu.VMEM((2, CHUNKS, length, nx * rows), bf16),
            pltpu.VMEM((2, nx * rows, length), bf16),
            pltpu.VMEM((2, nx * rows, length), bf16),
            pltpu.VMEM((length, length), f32),
            pltpu.VMEM((2, length, length), bf16),
            pltpu.SemaphoreType.DMA((3,)),
            pltpu.SemaphoreType.DMA((CHUNKS,)),
            pltpu.SemaphoreType.DMA((CHUNKS,)),
            pltpu.SemaphoreType.DMA((CHUNKS,)),
            pltpu.SemaphoreType.DMA((CHUNKS,)),
        ],
        compiler_params=pltpu.CompilerParams(
            collective_id=0, has_side_effects=True, vmem_limit_bytes=48 * 1024 * 1024
        ),
        cost_estimate=pl.CostEstimate(
            flops=24 * length**3, bytes_accessed=8 * force.size, transcendentals=0
        ),
    )(force, drag, jnp.asarray(table), jnp.asarray(turned), jnp.asarray(pieces))


def tables(row_pos, col_pos, length):
    phase = row_pos[:, None] * col_pos[None, :] % length
    angle = phase.astype(jnp.float32) * (2.0 * math.pi / length)
    return (jnp.cos(angle), jnp.sin(angle))


def green_block(drag, x_pos, y_pos, len_x, len_y):
    mode_x = jnp.where(x_pos < len_x // 2, x_pos, x_pos - len_x).astype(jnp.float32)
    mode_y = jnp.where(y_pos < len_y // 2, y_pos, y_pos - len_y).astype(jnp.float32)
    square = mode_x[:, None] ** 2 + mode_y[None, :] ** 2
    project = 1.0 - mode_x[:, None] ** 2 / jnp.maximum(square, 1.0)
    denom = drag[:, None, None] + 16.0 / (len_x * len_y) * square[None, :, :]
    return project[None, :, :] / denom


def swap_x(stacked, sign):

    def work(piece):
        length = piece.shape[2]
        index = lax.iota(jnp.int32, length)
        cosine, sine_tab = tables(index, index, length)
        first = piece[0]
        if piece.shape[0] == 2:
            second = piece[1]
            real_part = jnp.einsum(
                "kx,zxq->zkq", cosine, first, precision=HIGH
            ) - sign * jnp.einsum("kx,zxq->zkq", sine_tab, second, precision=HIGH)
            imag_part = sign * jnp.einsum(
                "kx,zxq->zkq", sine_tab, first, precision=HIGH
            ) + jnp.einsum("kx,zxq->zkq", cosine, second, precision=HIGH)
        else:
            real_part = jnp.einsum("kx,zxq->zkq", cosine, first, precision=HIGH)
            imag_part = sign * jnp.einsum("kx,zxq->zkq", sine_tab, first, precision=HIGH)
        outgoing = jnp.stack([real_part, imag_part], 0)
        return lax.all_to_all(outgoing, "gx", split_axis=2, concat_axis=3, tiled=True)

    return work(lax.all_to_all(stacked, "gx", split_axis=3, concat_axis=2, tiled=True))


def swap_y(stacked, sign, keep_imag):

    def work(piece):
        length = piece.shape[3]
        index = lax.iota(jnp.int32, length)
        cosine, sine_tab = tables(index, index, length)
        first = piece[0]
        second = piece[1]
        real_part = jnp.einsum("ky,zpy->zpk", cosine, first, precision=HIGH) - sign * jnp.einsum(
            "ky,zpy->zpk", sine_tab, second, precision=HIGH
        )
        if keep_imag:
            imag_part = sign * jnp.einsum(
                "ky,zpy->zpk", sine_tab, first, precision=HIGH
            ) + jnp.einsum("ky,zpy->zpk", cosine, second, precision=HIGH)
            outgoing = jnp.stack([real_part, imag_part], 0)
        else:
            outgoing = real_part[None]
        return lax.all_to_all(outgoing, "gy", split_axis=3, concat_axis=2, tiled=True)

    return work(lax.all_to_all(stacked, "gy", split_axis=2, concat_axis=3, tiled=True))


def on_device(force, drag):
    planes, width_x, width_y = force.shape
    len_x = width_x * lax.axis_size("gx")
    len_y = width_y * lax.axis_size("gy")
    whole_planes = planes == lax.axis_size("gx") * lax.axis_size("gy") and len_x == len_y
    if whole_planes and width_x % (16 * CHUNKS) == 0 and width_y % TILE == 0:
        return by_planes(force, drag)
    x_pos = lax.axis_index("gx") * width_x + lax.iota(jnp.int32, width_x)
    y_pos = lax.axis_index("gy") * width_y + lax.iota(jnp.int32, width_y)
    spectrum = swap_x(force[None], -1.0)
    green = green_block(drag, x_pos, y_pos, len_x, len_y)
    spectrum = swap_y(spectrum, -1.0, True)
    scaled = spectrum * green[None]
    inverse = swap_x(scaled, 1.0)
    inverse = swap_y(inverse, 1.0, False)
    result = inverse[0] * (1.0 / (len_x * len_y))
    return result


def solution(mesh):
    placed = (P(None, "gx", "gy"), P())
    return jax.shard_map(
        on_device, mesh=mesh, in_specs=placed, out_specs=P(None, "gx", "gy"), check_vma=False
    )
```

```python
import functools
import math

import jax
import jax.numpy as jnp
import numpy as np
from jax import lax
from jax.experimental import pallas as pl
from jax.experimental.pallas import tpu as pltpu
from jax.sharding import PartitionSpec as P

HIGH = lax.Precision.HIGHEST
MESH = pl.DeviceIdType.MESH
CHUNKS = 8
TILE = 256
WIDE = 512


def real_modes(length):
    half = length // 2
    row = np.arange(length)
    mode = np.where(row <= half, row, row - half)
    phase = np.outer(mode, np.arange(length)) % length
    angle = phase * (2.0 * np.pi / length)
    table = np.where((row <= half)[:, None], np.cos(angle), np.sin(angle))
    weight = np.where((row == 0) | (row == half), 1.0, 2.0) / length
    return table * np.sqrt(weight)[:, None]


def two_parts(table):
    high = table.astype(jnp.bfloat16)
    low = (table - high.astype(np.float64)).astype(jnp.bfloat16)
    return high, low


def split(value):
    high = value.astype(jnp.bfloat16)
    return high, (value - high.astype(jnp.float32)).astype(jnp.bfloat16)


def product(a_high, a_low, b_high, b_low):
    dot = functools.partial(jnp.dot, preferred_element_type=jnp.float32)
    return dot(a_high, b_high) + (dot(a_high, b_low) + dot(a_low, b_high))


def plane_kernel(
    nx, ny, force, drag, tables_in, turned_in, pieces_in, out, plane, green, table, turned, pieces, part, lines,
    total, modes,
    table_sem, send, recv, back_send, back_recv,
):
    gx, gy = lax.axis_index("gx"), lax.axis_index("gy")
    me = gx * ny + gy
    devices = nx * ny
    chunks, rows = plane.shape[1], plane.shape[2]
    width = force.shape[2]
    length = plane.shape[3]
    len_x = nx * chunks * rows
    count = nx * rows

    def peer(i):
        px = lax.rem(gx + (nx - 1 - lax.rem(i, nx)), nx)
        py = lax.rem(gy + (ny - 1 - i // nx), ny)
        return px, py

    def columns(j, size):
        return pl.ds(pl.multiple_of(j * size, size), size)

    def band(c):
        return pl.ds(pl.multiple_of(c * rows, rows), rows)

    loads = [
        pltpu.make_async_copy(tables_in, table, table_sem.at[0]),
        pltpu.make_async_copy(turned_in, turned, table_sem.at[1]),
        pltpu.make_async_copy(pieces_in, pieces, table_sem.at[2]),
    ]
    for load in loads:
        load.start()

    barrier = pltpu.get_barrier_semaphore()

    @pl.loop(0, devices - 1)
    def _(i):
        pl.semaphore_signal(barrier, inc=1, device_id=peer(i), device_id_type=MESH)

    pl.semaphore_wait(barrier, devices - 1)

    @pl.loop(0, chunks)
    def _(c):
        @pl.loop(0, devices - 1)
        def _(i):
            px, py = peer(i)
            pltpu.make_async_remote_copy(
                src_ref=force.at[px * ny + py, band(c)],
                dst_ref=plane.at[gx, c, :, columns(gy, width)],
                send_sem=send.at[c],
                recv_sem=recv.at[c],
                device_id=(px, py),
                device_id_type=MESH,
            ).start()

        pltpu.make_async_copy(
            force.at[me, band(c)], plane.at[gx, c, :, columns(gy, width)], recv.at[c]
        ).start()

    friction = drag[me]

    @pl.loop(0, len_x // TILE)
    def _(i):
        first = lax.broadcasted_iota(jnp.int32, (TILE, length), 0) + i * TILE
        second = lax.broadcasted_iota(jnp.int32, (TILE, length), 1)
        mode_x = jnp.where(first <= len_x // 2, first, first - len_x // 2).astype(jnp.float32)
        mode_y = jnp.where(second <= length // 2, second, second - length // 2).astype(jnp.float32)
        square_x = mode_x * mode_x
        square = square_x + mode_y * mode_y
        floor = jnp.maximum(square, 1.0)
        denom = friction + 16.0 / (len_x * length) * square
        total[columns(i, TILE), :] = jnp.zeros((TILE, length), jnp.float32)
        green[columns(i, TILE), :] = (floor - square_x) / (floor * denom)

    for load in loads:
        load.wait()

    def arrive(c, last):
        pltpu.make_async_copy(plane.at[:, c], plane.at[:, c], recv.at[c]).wait()
        high, low = split(plane[:, c].reshape(count, length))
        part[0] = high
        part[1] = low

        @pl.loop(0, length // WIDE)
        def _(j):
            cols = columns(j, WIDE)
            result = product(
                part[0],
                part[1],
                turned[0, :, :, :, cols].reshape(length, WIDE),
                turned[1, :, :, :, cols].reshape(length, WIDE),
            )
            high, low = split(result)
            lines[0, :, cols] = high
            lines[1, :, cols] = low

        @pl.loop(0, length // TILE)
        def _(j):
            cols = columns(j, TILE)

            @pl.loop(0, len_x // (2 * TILE))
            def _(i):
                band_i = columns(i, 2 * TILE)
                result = total[band_i, cols] + product(
                    pieces[0, c, band_i, :], pieces[1, c, band_i, :], lines[0, :, cols], lines[1, :, cols]
                )
                if last:
                    high, low = split(result * green[band_i, cols])
                    modes[0, band_i, cols] = high
                    modes[1, band_i, cols] = low
                else:
                    total[band_i, cols] = result

    @pl.loop(0, chunks - 1)
    def _(c):
        arrive(c, False)

    arrive(chunks - 1, True)

    @pl.loop(0, chunks)
    def _(c):
        @pl.loop(0, length // WIDE)
        def _(j):
            cols = columns(j, WIDE)
            result = product(
                turned[0, :, c].reshape(count, len_x),
                turned[1, :, c].reshape(count, len_x),
                modes[0, :, cols],
                modes[1, :, cols],
            )
            high, low = split(result)
            part[0, :, cols] = high
            part[1, :, cols] = low

        @pl.loop(0, length // WIDE)
        def _(j):
            cols = columns(j, WIDE)
            result = product(part[0], part[1], table[0, :, cols], table[1, :, cols])
            plane[:, c, :, cols] = result.reshape(nx, rows, WIDE)

        @pl.loop(0, devices - 1)
        def _(i):
            px, py = peer(i)
            pltpu.make_async_remote_copy(
                src_ref=plane.at[px, c, :, columns(py, width)],
                dst_ref=out.at[me, band(c)],
                send_sem=back_send.at[c],
                recv_sem=back_recv.at[c],
                device_id=(px, py),
                device_id_type=MESH,
            ).start()

        pltpu.make_async_copy(
            plane.at[gx, c, :, columns(gy, width)], out.at[me, band(c)], back_recv.at[c]
        ).start()

    @pl.loop(0, chunks)
    def _(c):
        sent = force.at[pl.ds(0, devices - 1), band(c)]
        pltpu.make_async_copy(sent, sent, send.at[c]).wait()
        pltpu.make_async_copy(sent, sent, back_send.at[c]).wait()
        landed = out.at[:, band(c)]
        pltpu.make_async_copy(landed, landed, back_recv.at[c]).wait()


def by_planes(force, drag):
    nx, ny = lax.axis_size("gx"), lax.axis_size("gy")
    planes, width_x, width_y = force.shape
    length = width_x * nx
    rows = width_x // CHUNKS
    modes = real_modes(length)
    table = np.stack(two_parts(modes))
    turned = np.stack(two_parts(modes.T)).reshape(2, nx, CHUNKS, rows, length)
    pieces = table.reshape(2, length, nx, CHUNKS, rows).transpose(0, 3, 1, 2, 4).reshape(2, CHUNKS, length, nx * rows)
    anywhere = pl.BlockSpec(memory_space=pl.ANY)
    bf16, f32 = jnp.bfloat16, jnp.float32
    return pl.pallas_call(
        functools.partial(plane_kernel, nx, ny),
        out_shape=jax.ShapeDtypeStruct(force.shape, force.dtype),
        in_specs=[anywhere, pl.BlockSpec(memory_space=pltpu.SMEM), anywhere, anywhere, anywhere],
        out_specs=anywhere,
        scratch_shapes=[
            pltpu.VMEM((nx, CHUNKS, rows, length), f32),
            pltpu.VMEM((length, length), f32),
            pltpu.VMEM((2, length, length), bf16),
            pltpu.VMEM((2, nx, CHUNKS, rows, length), bf16),
            pltpu.VMEM((2, CHUNKS, length, nx * rows), bf16),
            pltpu.VMEM((2, nx * rows, length), bf16),
            pltpu.VMEM((2, nx * rows, length), bf16),
            pltpu.VMEM((length, length), f32),
            pltpu.VMEM((2, length, length), bf16),
            pltpu.SemaphoreType.DMA((3,)),
            pltpu.SemaphoreType.DMA((CHUNKS,)),
            pltpu.SemaphoreType.DMA((CHUNKS,)),
            pltpu.SemaphoreType.DMA((CHUNKS,)),
            pltpu.SemaphoreType.DMA((CHUNKS,)),
        ],
        compiler_params=pltpu.CompilerParams(
            collective_id=0, has_side_effects=True, vmem_limit_bytes=48 * 1024 * 1024
        ),
        cost_estimate=pl.CostEstimate(
            flops=24 * length**3, bytes_accessed=8 * force.size, transcendentals=0
        ),
    )(force, drag, jnp.asarray(table), jnp.asarray(turned), jnp.asarray(pieces))


def tables(row_pos, col_pos, length):
    phase = row_pos[:, None] * col_pos[None, :] % length
    angle = phase.astype(jnp.float32) * (2.0 * math.pi / length)
    return (jnp.cos(angle), jnp.sin(angle))


def green_block(drag, x_pos, y_pos, len_x, len_y):
    mode_x = jnp.where(x_pos < len_x // 2, x_pos, x_pos - len_x).astype(jnp.float32)
    mode_y = jnp.where(y_pos < len_y // 2, y_pos, y_pos - len_y).astype(jnp.float32)
    square = mode_x[:, None] ** 2 + mode_y[None, :] ** 2
    project = 1.0 - mode_x[:, None] ** 2 / jnp.maximum(square, 1.0)
    denom = drag[:, None, None] + 16.0 / (len_x * len_y) * square[None, :, :]
    return project[None, :, :] / denom


def swap_x(stacked, sign):

    def work(piece):
        length = piece.shape[2]
        index = lax.iota(jnp.int32, length)
        cosine, sine_tab = tables(index, index, length)
        first = piece[0]
        if piece.shape[0] == 2:
            second = piece[1]
            real_part = jnp.einsum(
                "kx,zxq->zkq", cosine, first, precision=HIGH
            ) - sign * jnp.einsum("kx,zxq->zkq", sine_tab, second, precision=HIGH)
            imag_part = sign * jnp.einsum(
                "kx,zxq->zkq", sine_tab, first, precision=HIGH
            ) + jnp.einsum("kx,zxq->zkq", cosine, second, precision=HIGH)
        else:
            real_part = jnp.einsum("kx,zxq->zkq", cosine, first, precision=HIGH)
            imag_part = sign * jnp.einsum("kx,zxq->zkq", sine_tab, first, precision=HIGH)
        outgoing = jnp.stack([real_part, imag_part], 0)
        return lax.all_to_all(outgoing, "gx", split_axis=2, concat_axis=3, tiled=True)

    return work(lax.all_to_all(stacked, "gx", split_axis=3, concat_axis=2, tiled=True))


def swap_y(stacked, sign, keep_imag):

    def work(piece):
        length = piece.shape[3]
        index = lax.iota(jnp.int32, length)
        cosine, sine_tab = tables(index, index, length)
        first = piece[0]
        second = piece[1]
        real_part = jnp.einsum("ky,zpy->zpk", cosine, first, precision=HIGH) - sign * jnp.einsum(
            "ky,zpy->zpk", sine_tab, second, precision=HIGH
        )
        if keep_imag:
            imag_part = sign * jnp.einsum(
                "ky,zpy->zpk", sine_tab, first, precision=HIGH
            ) + jnp.einsum("ky,zpy->zpk", cosine, second, precision=HIGH)
            outgoing = jnp.stack([real_part, imag_part], 0)
        else:
            outgoing = real_part[None]
        return lax.all_to_all(outgoing, "gy", split_axis=3, concat_axis=2, tiled=True)

    return work(lax.all_to_all(stacked, "gy", split_axis=2, concat_axis=3, tiled=True))


def on_device(force, drag):
    planes, width_x, width_y = force.shape
    len_x = width_x * lax.axis_size("gx")
    len_y = width_y * lax.axis_size("gy")
    whole_planes = planes == lax.axis_size("gx") * lax.axis_size("gy") and len_x == len_y
    if whole_planes and width_x % (16 * CHUNKS) == 0 and width_y % TILE == 0 and len_y % WIDE == 0:
        return by_planes(force, drag)
    x_pos = lax.axis_index("gx") * width_x + lax.iota(jnp.int32, width_x)
    y_pos = lax.axis_index("gy") * width_y + lax.iota(jnp.int32, width_y)
    spectrum = swap_x(force[None], -1.0)
    green = green_block(drag, x_pos, y_pos, len_x, len_y)
    spectrum = swap_y(spectrum, -1.0, True)
    scaled = spectrum * green[None]
    inverse = swap_x(scaled, 1.0)
    inverse = swap_y(inverse, 1.0, False)
    result = inverse[0] * (1.0 / (len_x * len_y))
    return result


def solution(mesh):
    placed = (P(None, "gx", "gy"), P())
    return jax.shard_map(
        on_device, mesh=mesh, in_specs=placed, out_specs=P(None, "gx", "gy"), check_vma=False
    )
```
